32 devices in a mesh: aln: 4 (over x, core), seq: 8 (over z, y).
Axes of the slice: x: 2, y: 2, z: 4, core: 2. Of those that a mesh axis runs over, the one named last changes fastest.
Arguments:
- embedded_homologs: bfloat16 [256, 128, 768], P(('aln', 'seq')), parts along dimension 0, may hold values from -6 to 6
- homolog_tallies: int32 [4], P('aln'), parts along dimension 0, may hold values from 16 to 64
- horizontal_probe_matrix: bfloat16 [768, 768], replicated
- horizontal_lookup_matrix: bfloat16 [768, 768], replicated
- horizontal_content_matrix: bfloat16 [768, 768], replicated, may hold values from -0.21875 to 0.21875
- vertical_probe_matrix: bfloat16 [768, 768], replicated
- vertical_lookup_matrix: bfloat16 [768, 768], replicated
- vertical_content_matrix: bfloat16 [768, 768], replicated, may hold values from -0.21875 to 0.21875
Outputs:
- row_output: bfloat16 [256, 128, 768], P(('aln', 'seq')), parts along dimension 0
- column_output: bfloat16 [256, 128, 768], P(('aln', 'seq')), parts along dimension 0
The draws below stay inside these ranges and needn't reach their ends.
There are 4 independent parts, one for each index of `aln`. The reference program is written for one: setup_inputs(seed, part) draws one part's arguments, and reference() takes and returns one part's arrays. A program takes and returns all parts, laid end to end along the dimension named above; an argument that names none is the same for every part. Nothing has to cross between parts.
Inputs may be any that keep to these rules, and one draw needn't show every extreme that they name: Sequence slots from homolog_tallies[0] on are padding.
All inputs are finite; a program needn't handle non-finite values.
Results may differ from the reference program's by a relative error of at most 0.024.
Values may be sent and summed in bfloat16 or wider, within the bound.
A program may use at most 128 MiB of HBM per device.

```python
import jax
import jax.numpy as jnp
from jax import lax

EMBED_DIMENSION = 768
H = 12
DH = 64
POSITION_TOTAL = 128
HOMOLOG_CAPACITY = 64


def paired_weights(key, salt):
    base = jax.random.fold_in(key, salt)
    first = jax.random.normal(jax.random.fold_in(base, 1), (EMBED_DIMENSION, EMBED_DIMENSION), jnp.float32) / jnp.sqrt(jnp.float32(EMBED_DIMENSION))
    other = jax.random.normal(jax.random.fold_in(base, 2), (EMBED_DIMENSION, EMBED_DIMENSION), jnp.float32) / jnp.sqrt(jnp.float32(EMBED_DIMENSION))
    second = other
    return (first, second)


def draw_horizontal_probe_matrix(key, part):
    return paired_weights(key, 11)[0].astype(jnp.bfloat16)


def draw_horizontal_lookup_matrix(key, part):
    return paired_weights(key, 11)[1].astype(jnp.bfloat16)


def draw_vertical_probe_matrix(key, part):
    return paired_weights(key, 23)[0].astype(jnp.bfloat16)


def draw_vertical_lookup_matrix(key, part):
    return paired_weights(key, 23)[1].astype(jnp.bfloat16)


def block_levels(rng, extent, shards, least, largest):
    loudness = 1.0
    for axis_at, parts in shards:
        draws = jax.random.uniform(jax.random.fold_in(jax.random.fold_in(rng, 6), axis_at), (parts,), jnp.float32, least / len(shards), largest / len(shards))
        loudness = loudness * jnp.repeat(jnp.exp(draws), extent[axis_at] // parts).reshape((-1,) + (1,) * (len(extent) - 1 - axis_at))
    return loudness


def gaussian(stream_key, dims, width, reach, split=(), kind=jnp.bfloat16):
    level = block_levels(stream_key, dims, split, -0.22, 0.18) if split else 1.0
    values = jax.random.normal(stream_key, dims, jnp.float32) * width * level
    return jnp.minimum(jnp.maximum(values, -reach), reach).astype(kind)


def setup_inputs(seed: int = 0, part: int = 0) -> dict:
    streams_of = jax.random.split(jax.random.key(seed), 9)
    part_keys = jax.random.split(jax.random.fold_in(streams_of[8], part), 9)
    return {
        "embedded_homologs": gaussian(part_keys[0], (HOMOLOG_CAPACITY, POSITION_TOTAL, EMBED_DIMENSION), 1.0, 6.0, ((0, 8),)),
        "homolog_tallies": jax.random.randint(part_keys[1], (1,), HOMOLOG_CAPACITY // 4, HOMOLOG_CAPACITY + 1).astype(jnp.int32),
        "horizontal_probe_matrix": draw_horizontal_probe_matrix(jax.random.fold_in(streams_of[8], 71), part),
        "horizontal_lookup_matrix": draw_horizontal_lookup_matrix(jax.random.fold_in(streams_of[8], 71), part),
        "horizontal_content_matrix": gaussian(streams_of[4], (EMBED_DIMENSION, EMBED_DIMENSION), EMBED_DIMENSION ** -0.5, 0.21875),
        "vertical_probe_matrix": draw_vertical_probe_matrix(jax.random.fold_in(streams_of[8], 71), part),
        "vertical_lookup_matrix": draw_vertical_lookup_matrix(jax.random.fold_in(streams_of[8], 71), part),
        "vertical_content_matrix": gaussian(streams_of[7], (EMBED_DIMENSION, EMBED_DIMENSION), EMBED_DIMENSION ** -0.5, 0.21875),
    }


def standardize_features(values):
    centre = lax.optimization_barrier(jnp.mean(values, axis=-1, keepdims=True))
    spread = lax.optimization_barrier(jnp.mean((values - centre) ** 2, axis=-1, keepdims=True))
    return (values - centre) * lax.rsqrt(spread + 1e-05)

def project(standardized_activations, weight):
    flat = standardized_activations.reshape(HOMOLOG_CAPACITY * POSITION_TOTAL, EMBED_DIMENSION)
    return jnp.dot(flat, weight, preferred_element_type=jnp.float32).astype(jnp.bfloat16).reshape(HOMOLOG_CAPACITY, POSITION_TOTAL, H, DH)

def column_one(pieces, livef):
    query, key_rows, value_rows = pieces
    scores = jnp.einsum('shd,thd->hst', query.astype(jnp.float32), key_rows.astype(jnp.float32)) / jnp.sqrt(jnp.float32(DH))
    scores = jnp.where(livef[None, None, :] > 0, scores, jnp.float32(-1e+30))
    weights = jax.nn.softmax(scores, axis=-1).astype(jnp.bfloat16)
    result = jnp.einsum('hst,thd->shd', weights.astype(jnp.float32), value_rows.astype(jnp.float32))
    return (result * livef[:, None, None]).astype(jnp.bfloat16)

def reference(embedded_homologs, homolog_tallies, horizontal_probe_matrix, horizontal_lookup_matrix, horizontal_content_matrix, vertical_probe_matrix, vertical_lookup_matrix, vertical_content_matrix):
    count = homolog_tallies[0]
    livef = (jnp.arange(HOMOLOG_CAPACITY, dtype=jnp.int32) < count).astype(jnp.float32)
    standardized_activations = standardize_features(embedded_homologs.astype(jnp.float32)).astype(jnp.bfloat16)
    rq = project(standardized_activations, horizontal_probe_matrix)
    rk = project(standardized_activations, horizontal_lookup_matrix)
    rv = project(standardized_activations, horizontal_content_matrix)
    masked = rq.astype(jnp.float32) * livef[:, None, None, None]
    logits = jnp.einsum('sihd,sjhd->hij', masked, rk.astype(jnp.float32))
    logits = logits / (jnp.sqrt(jnp.float32(DH)) * jnp.sqrt(count.astype(jnp.float32)))
    weights = jax.nn.softmax(logits, axis=-1).astype(jnp.bfloat16)
    horizontal_mixing_result = jnp.einsum('hij,sjhd->sihd', weights.astype(jnp.float32), rv.astype(jnp.float32))
    horizontal_mixing_result = (horizontal_mixing_result * livef[:, None, None, None]).astype(jnp.bfloat16).reshape(HOMOLOG_CAPACITY, POSITION_TOTAL, EMBED_DIMENSION)
    intermediate_activations = embedded_homologs.astype(jnp.float32) + horizontal_mixing_result.astype(jnp.float32)
    normed2 = standardize_features(intermediate_activations).astype(jnp.bfloat16)
    cq = jnp.moveaxis(project(normed2, vertical_probe_matrix), 1, 0)
    ck = jnp.moveaxis(project(normed2, vertical_lookup_matrix), 1, 0)
    cv = jnp.moveaxis(project(normed2, vertical_content_matrix), 1, 0)
    columns = lax.map(lambda pieces: column_one(pieces, livef), (cq, ck, cv))
    column_out = jnp.moveaxis(columns, 0, 1).reshape(HOMOLOG_CAPACITY, POSITION_TOTAL, EMBED_DIMENSION)
    return (horizontal_mixing_result, column_out)
```

```python
import functools

import jax
import jax.numpy as jnp
import numpy as np
from jax import lax
from jax.experimental import pallas as pl
from jax.experimental.pallas import tpu as pltpu
from jax.sharding import PartitionSpec as P

DH = 64
PAIR = 2 * DH
GROUP = 2 * PAIR
F32 = jnp.float32
BF16 = jnp.bfloat16
MESH = pl.DeviceIdType.MESH


def standardize(values):
    centre = jnp.mean(values, axis=-1, keepdims=True)
    shifted = values - centre
    spread = jnp.mean(shifted * shifted, axis=-1, keepdims=True)
    return shifted * lax.rsqrt(spread + 1e-05)


def softmax(scores):
    e = jnp.exp(scores - jnp.max(scores, axis=-1, keepdims=True))
    return (e * (1.0 / jnp.sum(e, axis=-1, keepdims=True))).astype(BF16)


def dot(a, b):
    return jnp.dot(a, b, preferred_element_type=F32)


def dot_t(a, b):
    return lax.dot_general(a, b, (((1,), (1,)), ((), ())), preferred_element_type=F32)


def kernel(
    n, seqs, length, width,
    count_ref, inv_ref, x_hbm, hq_hbm, hk_hbm, hv_hbm, vq_hbm, vk_hbm, vv_hbm, there_hbm, back_hbm,
    row_hbm, col_hbm,
    x, hq, hk, hv, vq, vk, vv, there, back,
    normed, rq, rk, rv, part, part_in, weights, row_out, send, arrived, cq, ck, cv, ret, ret_in, out,
    load_sem, rs_s, rs_r, ag_s, ag_r, go_s, go_r, re_s, re_r,
):
    per = length // n
    rows = seqs * length
    block = seqs * per
    pair_rows = 2 * seqs
    pairs = per // 2
    step_pairs = min(2, pairs)
    steps = pairs // step_pairs
    step_rows = step_pairs * pair_rows
    span = n * pair_rows
    groups = width // GROUP
    group_rows = (GROUP // DH) * length
    share = group_rows // n
    me = lax.axis_index("seq")
    count = count_ref[0]
    inverse = inv_ref[0]

    loads = [
        pltpu.make_async_copy(src, dst, load_sem.at[at])
        for at, (src, dst) in enumerate(
            [(x_hbm, x), (hq_hbm, hq), (hk_hbm, hk), (hv_hbm, hv), (there_hbm, there),
             (vq_hbm, vq), (vk_hbm, vk), (vv_hbm, vv), (back_hbm, back)]
        )
    ]
    for load in loads:
        load.start()

    barrier = pltpu.get_barrier_semaphore()

    def greet(k, c):
        pl.semaphore_signal(
            barrier, inc=1, device_id={"seq": lax.rem(me + k, n)}, device_id_type=MESH
        )
        return c

    lax.fori_loop(1, n, greet, 0)

    def target(k):
        return lax.rem(me + k, n)

    def source(k):
        return lax.rem(me + n - k, n)

    def aligned(index, size):
        return pl.ds(pl.multiple_of(index * size, size), size)

    def remote(src, dst, s, r, to):
        return pltpu.make_async_remote_copy(
            src_ref=src, dst_ref=dst, send_sem=s, recv_sem=r, device_id={"seq": to},
            device_id_type=MESH,
        )

    def rs_copy(g, k):
        return remote(
            part.at[g, aligned(target(k), share)], part_in.at[g, k], rs_s.at[g, k], rs_r.at[g, k],
            target(k),
        )

    def ag_copy(g, k, owner):
        at = aligned(owner, share)
        return remote(
            weights.at[g, at], weights.at[g, at], ag_s.at[g, k], ag_r.at[g, k], target(k)
        )

    def go_copy(t, k, owner):
        at = aligned(t, step_rows)
        return remote(
            send.at[target(k), at], arrived.at[owner, at], go_s.at[t, k], go_r.at[t, k], target(k)
        )

    def re_copy(t, k, owner):
        at = aligned(t, step_rows)
        return remote(
            ret.at[target(k), at], ret_in.at[owner, at], re_s.at[t, k], re_r.at[t, k], target(k)
        )

    lane = lax.broadcasted_iota(jnp.int32, (1, PAIR), 1)
    left = jnp.where(lane < DH, 1.0, 0.0).astype(BF16)
    right = jnp.where(lane < DH, 0.0, 1.0).astype(BF16)

    loads[0].wait()

    def norm_one(s, c):
        at = aligned(s, length)
        normed[at] = standardize(x[s].astype(F32)).astype(BF16)
        return c

    lax.fori_loop(0, seqs, norm_one, 0)
    loads[1].wait()
    loads[2].wait()

    def side(ref, lanes):
        return jnp.concatenate(
            [ref[s * length:(s + 1) * length, lanes] for s in range(seqs)], axis=1
        )

    tile = 2 * length
    for g in range(groups):
        lanes = slice(g * GROUP, (g + 1) * GROUP)

        def project(r, c, lanes=lanes):
            at = aligned(r, tile)
            a = normed[at]
            slot = lax.broadcasted_iota(jnp.int32, (tile, 1), 0)
            first = me * seqs + r * 2
            live = jnp.where(
                jnp.where(slot < length, first, first + 1) < count, 1.0, 0.0
            ).astype(F32)
            rq[at, lanes] = (dot(a, hq[:, lanes]) * live).astype(BF16)
            rk[at, lanes] = dot(a, hk[:, lanes]).astype(BF16)
            return c

        lax.fori_loop(0, rows // tile, project, 0)
        left_s = jnp.concatenate([left] * seqs, axis=1)
        right_s = jnp.concatenate([right] * seqs, axis=1)
        for p in range(GROUP // PAIR):
            pl_lanes = slice(g * GROUP + p * PAIR, g * GROUP + (p + 1) * PAIR)
            q = side(rq, pl_lanes)
            q2 = jnp.concatenate([q * left_s, q * right_s], axis=0)
            part[g, p * 2 * length:(p + 1) * 2 * length, :] = dot_t(q2, side(rk, pl_lanes)).astype(BF16)
        if g == 0:
            pl.semaphore_wait(barrier, n - 1)

        def rs_start(k, c, g=g):
            rs_copy(g, k).start()
            return c

        lax.fori_loop(1, n, rs_start, 0)

    loads[3].wait()

    def project_v(r, c):
        at = aligned(r, tile)
        rv[at] = dot(normed[at], hv[...]).astype(BF16)
        return c

    lax.fori_loop(0, rows // tile, project_v, 0)

    for g in range(groups):
        def add(k, total, g=g):
            rs_copy(g, k).wait_recv()
            return total + part_in[g, k].astype(F32)

        logits = lax.fori_loop(1, n, add, part[g, aligned(me, share), :].astype(F32))
        weights[g, aligned(me, share), :] = softmax(logits * inverse)

        def ag_start(k, c, g=g):
            ag_copy(g, k, me).start()
            return c

        lax.fori_loop(1, n, ag_start, 0)

    for g in range(groups):
        def ag_wait(k, c, g=g):
            ag_copy(g, k, source(k)).wait_recv()
            return c

        lax.fori_loop(1, n, ag_wait, 0)
        left_s = jnp.concatenate([left] * seqs, axis=1)
        right_s = jnp.concatenate([right] * seqs, axis=1)
        for p in range(GROUP // PAIR):
            lanes = slice(g * GROUP + p * PAIR, g * GROUP + (p + 1) * PAIR)
            w2 = jnp.concatenate(
                [weights[g, (2 * p + i) * length:(2 * p + i + 1) * length, :] for i in range(2)],
                axis=1,
            )
            v = side(rv, lanes)
            mixed = dot(w2, jnp.concatenate([v * left_s, v * right_s], axis=0))
            for s in range(seqs):
                live = jnp.where(me * seqs + s < count, 1.0, 0.0).astype(F32)
                row_out[s, :, lanes] = (mixed[:, s * PAIR:(s + 1) * PAIR] * live).astype(BF16)

    row_copy = pltpu.make_async_copy(row_out, row_hbm, load_sem.at[len(loads)])
    row_copy.start()

    loads[4].wait()
    if per % 16 == 0:
        for d in range(n):
            at = slice(d * per, (d + 1) * per)
            a = x[:, at, :].astype(F32) + row_out[:, at, :].astype(F32)
            a = standardize(a).astype(BF16).reshape(block, width)
            send[d] = dot(there[...], a).astype(BF16)
    else:
        def norm_two(s, c):
            normed[aligned(s, length)] = standardize(
                x[s].astype(F32) + row_out[s].astype(F32)
            ).astype(BF16)
            return c

        lax.fori_loop(0, seqs, norm_two, 0)
        for d in range(n):
            send[d] = dot(there[d * block:(d + 1) * block, :], normed[...]).astype(BF16)

    def go_step(t, c):
        def go_start(k, c):
            go_copy(t, k, me).start()
            return c

        return lax.fori_loop(1, n, go_start, c)

    lax.fori_loop(0, steps, go_step, 0)
    arrived[me] = send[me]
    for load in loads[5:]:
        load.wait()

    shift = seqs.bit_length() - 1
    shape = (2 * span, span)

    def place(index):
        return lax.shift_left(lax.shift_right_logical(index, shift + 1), shift) + (index & (seqs - 1))

    def column(index):
        return lax.shift_right_logical(index, shift) & 1

    key = lax.broadcasted_iota(jnp.int32, shape, 1)
    query = lax.broadcasted_iota(jnp.int32, shape, 0)
    open_f = jnp.where(
        (column(key) == column(query)) & (place(key) < count), 1.0, 0.0
    )
    live_q = jnp.where(
        place(lax.broadcasted_iota(jnp.int32, (span, 1), 0)) < count, 1.0, 0.0
    ).astype(F32)

    def attend_step(t, c):
        def go_wait(k, c):
            go_copy(t, k, source(k)).wait_recv()
            return c

        lax.fori_loop(1, n, go_wait, 0)
        a = jnp.concatenate(
            [
                arrived[:, pl.ds(pl.multiple_of(t * step_rows + p * pair_rows, pair_rows), pair_rows), :]
                .reshape(span, width)
                for p in range(step_pairs)
            ],
            axis=0,
        )
        cq[...] = (dot(a, vq[...]) * (DH ** -0.5)).astype(BF16)
        ck[...] = dot(a, vk[...]).astype(BF16)
        cv[...] = dot(a, vv[...]).astype(BF16)

        def attend_pair(p, c):
            at = aligned(p, span)
            out_at = pl.ds(
                pl.multiple_of(t * step_rows + p * pair_rows, pair_rows), pair_rows
            )
            for h in range(width // PAIR):
                lanes = slice(h * PAIR, (h + 1) * PAIR)
                q = cq[at, lanes]
                scores = dot_t(jnp.concatenate([q * left, q * right], axis=0), ck[at, lanes])
                w = softmax(jnp.where(open_f > 0.5, scores, -1e30))
                w2 = jnp.concatenate([w[:span], w[span:]], axis=1)
                v = cv[at, lanes]
                o = dot(w2, jnp.concatenate([v * left, v * right], axis=0))
                ret[:, out_at, lanes] = (o * live_q).astype(BF16).reshape(n, pair_rows, PAIR)
            return c

        lax.fori_loop(0, step_pairs, attend_pair, 0)

        def re_start(k, c):
            re_copy(t, k, me).start()
            return c

        return lax.fori_loop(1, n, re_start, c)

    lax.fori_loop(0, steps, attend_step, 0)
    ret_in[me] = ret[me]

    def re_wait(t, c):
        def one(k, c):
            re_copy(t, k, source(k)).wait_recv()
            return c

        return lax.fori_loop(1, n, one, c)

    lax.fori_loop(0, steps, re_wait, 0)
    if per % 16 == 0:
        for d in range(n):
            out[:, d * per:(d + 1) * per, :] = (
                dot(back[...], ret_in[d]).astype(BF16).reshape(seqs, per, width)
            )
    else:
        flat = ret_in[...].reshape(n * block, width)
        for s in range(seqs):
            out[s] = dot(back[s * length:(s + 1) * length, :], flat).astype(BF16)
    col_copy = pltpu.make_async_copy(out, col_hbm, load_sem.at[len(loads) + 1])
    col_copy.start()

    def sent(k, c):
        for g in range(groups):
            rs_copy(g, k).wait_send()
            ag_copy(g, k, me).wait_send()
        for t in range(steps):
            go_copy(t, k, me).wait_send()
            re_copy(t, k, me).wait_send()
        return c

    lax.fori_loop(1, n, sent, 0)
    row_copy.wait()
    col_copy.wait()


def local(x, tallies, hq, hk, hv, vq, vk, vv):
    seqs, length, width = x.shape
    n = lax.axis_size("seq")
    per = length // n
    block = seqs * per
    groups = width // GROUP
    share = (GROUP // DH) * length // n
    pairs = per // 2
    step_pairs = min(2, pairs)
    steps = pairs // step_pairs
    span = n * 2 * seqs
    if per % 16 == 0:
        order = np.arange(block).reshape(seqs, per).T.reshape(-1)
    else:
        order = np.arange(n * block).reshape(seqs, n, per).transpose(1, 2, 0).reshape(-1)
    there = np.zeros((order.size, order.size), np.float32)
    there[np.arange(order.size), order] = 1.0
    inverse = 1.0 / (jnp.sqrt(F32(DH)) * jnp.sqrt(tallies.astype(F32)))
    any_spec = pl.BlockSpec(memory_space=pl.ANY)
    smem_spec = pl.BlockSpec(memory_space=pltpu.SMEM)
    rows = seqs * length

    def vmem(*shape):
        return pltpu.VMEM(shape, BF16)

    def dma(*shape):
        return pltpu.SemaphoreType.DMA(shape)

    return pl.pallas_call(
        functools.partial(kernel, n, seqs, length, width),
        out_shape=(jax.ShapeDtypeStruct(x.shape, BF16), jax.ShapeDtypeStruct(x.shape, BF16)),
        in_specs=[smem_spec, smem_spec] + [any_spec] * 9,
        out_specs=(any_spec, any_spec),
        scratch_shapes=[
            vmem(*x.shape),
            *[vmem(width, width) for _ in range(6)],
            vmem(order.size, order.size),
            vmem(order.size, order.size),
            vmem(rows, width),
            vmem(rows, width),
            vmem(rows, width),
            vmem(rows, width),
            vmem(groups, n * share, length),
            vmem(groups, n, share, length),
            vmem(groups, n * share, length),
            vmem(*x.shape),
            vmem(n, block, width),
            vmem(n, block, width),
            vmem(step_pairs * span, width),
            vmem(step_pairs * span, width),
            vmem(step_pairs * span, width),
            vmem(n, block, width),
            vmem(n, block, width),
            vmem(*x.shape),
            dma(11),
            dma(groups, n), dma(groups, n), dma(groups, n), dma(groups, n),
            dma(steps, n), dma(steps, n), dma(steps, n), dma(steps, n),
        ],
        compiler_params=pltpu.CompilerParams(
            collective_id=0, has_side_effects=True, vmem_limit_bytes=56 * 1024 * 1024
        ),
    )(tallies, inverse, x, hq, hk, hv, vq, vk, vv, jnp.asarray(there, BF16), jnp.asarray(there.T, BF16))


def solution(mesh):
    in_specs = (P(("aln", "seq"), None, None), P("aln"), P(), P(), P(), P(), P(), P())
    out_specs = (P(("aln", "seq"), None, None), P(("aln", "seq"), None, None))
    return jax.shard_map(local, mesh=mesh, in_specs=in_specs, out_specs=out_specs, check_vma=False)
```

```python
import functools

import jax
import jax.numpy as jnp
import numpy as np
from jax import lax
from jax.experimental import pallas as pl
from jax.experimental.pallas import tpu as pltpu
from jax.sharding import PartitionSpec as P

DH = 64
PAIR = 2 * DH
GROUP = 2 * PAIR
STEP_PAIRS = 2
F32 = jnp.float32
BF16 = jnp.bfloat16
MESH = pl.DeviceIdType.MESH


def standardize(values):
    centre = jnp.mean(values, axis=-1, keepdims=True)
    shifted = values - centre
    spread = jnp.mean(shifted * shifted, axis=-1, keepdims=True)
    return shifted * lax.rsqrt(spread + 1e-05)


def softmax(scores):
    e = jnp.exp(scores - jnp.max(scores, axis=-1, keepdims=True))
    return (e * (1.0 / jnp.sum(e, axis=-1, keepdims=True))).astype(BF16)


def dot(a, b):
    return jnp.dot(a, b, preferred_element_type=F32)


def dot_t(a, b):
    return lax.dot_general(a, b, (((1,), (1,)), ((), ())), preferred_element_type=F32)


def kernel(
    n, seqs, length, width,
    count_ref, inv_ref, x_hbm, hq_hbm, hk_hbm, hv_hbm, vq_hbm, vk_hbm, vv_hbm, there_hbm, back_hbm,
    row_hbm, col_hbm,
    x, hq, hk, hv, vq, vk, vv, there, back,
    normed, rq, rk, rv, part, part_in, half_sum, half_in, weights, row_out,
    send, arrived, cq, ck, cv, ret, ret_in, out,
    load_sem, rs_s, rs_r, ex_s, ex_r, ag_s, ag_r, go_s, go_r, re_s, re_r,
):
    half = n // 2
    per = length // n
    rows = seqs * length
    pair_rows = 2 * seqs
    step_pairs = min(STEP_PAIRS, per // 2)
    steps = per // 2 // step_pairs
    step_rows = step_pairs * pair_rows
    step_columns = n * step_pairs * 2
    span = n * pair_rows
    groups = width // GROUP
    share = (GROUP // DH) * length // half
    me = lax.axis_index("seq")
    side_of_me = me // half
    place_of_me = lax.rem(me, half)
    count = count_ref[0]
    inverse = inv_ref[0]

    loads = [
        pltpu.make_async_copy(src, dst, load_sem.at[at])
        for at, (src, dst) in enumerate(
            [(x_hbm, x), (hq_hbm, hq), (hk_hbm, hk), (hv_hbm, hv), (there_hbm, there),
             (vq_hbm, vq), (vk_hbm, vk), (vv_hbm, vv), (back_hbm, back)]
        )
    ]
    for load in loads:
        load.start()

    barrier = pltpu.get_barrier_semaphore()

    def greet(k, c):
        pl.semaphore_signal(
            barrier, inc=1, device_id={"seq": lax.rem(me + k, n)}, device_id_type=MESH
        )
        return c

    lax.fori_loop(1, n, greet, 0)

    def target(k):
        side = lax.rem(side_of_me + 1 + k // half, 2)
        return side * half + lax.rem(place_of_me + k, half)

    def source(k):
        side = lax.rem(side_of_me + 1 + k // half, 2)
        return side * half + lax.rem(place_of_me + n - k, half)

    def aligned(index, size):
        return pl.ds(pl.multiple_of(index * size, size), size)

    def remote(src, dst, s, r, to):
        return pltpu.make_async_remote_copy(
            src_ref=src, dst_ref=dst, send_sem=s, recv_sem=r, device_id={"seq": to},
            device_id_type=MESH,
        )

    def each(body):
        def one(k, c):
            body(k)
            return c

        lax.fori_loop(0, half, one, 0)
        lax.fori_loop(half + 1, n, one, 0)

    def near(body):
        def one(j, c):
            body(j)
            return c

        lax.fori_loop(1, half, one, 0)

    def rs_copy(g, j):
        at = aligned(lax.rem(place_of_me + j, half), share)
        return remote(
            part.at[g, at], part_in.at[g, j], rs_s.at[g, j], rs_r.at[g, j], target(half + j)
        )

    def ex_copy(g):
        return remote(half_sum.at[g], half_in.at[g], ex_s.at[g], ex_r.at[g], target(0))

    def ag_copy(g, j, owner):
        at = aligned(lax.rem(owner, half), share)
        return remote(
            weights.at[g, at], weights.at[g, at], ag_s.at[g, j], ag_r.at[g, j], target(half + j)
        )

    def go_copy(t, k, owner):
        return remote(
            send.at[t, aligned(target(k), step_rows)], arrived.at[t, aligned(owner, step_rows)],
            go_s.at[t, k], go_r.at[t, k], target(k),
        )

    def re_copy(t, k, owner):
        return remote(
            ret.at[t, target(k)], ret_in.at[t, aligned(owner, step_rows)],
            re_s.at[t, k], re_r.at[t, k], target(k),
        )

    lane = lax.broadcasted_iota(jnp.int32, (1, PAIR), 1)
    left = jnp.where(lane < DH, 1.0, 0.0).astype(BF16)
    right = jnp.where(lane < DH, 0.0, 1.0).astype(BF16)
    left_s = jnp.concatenate([left] * seqs, axis=1)
    right_s = jnp.concatenate([right] * seqs, axis=1)

    loads[0].wait()

    def norm_one(s, c):
        normed[aligned(s, length)] = standardize(x[s].astype(F32)).astype(BF16)
        return c

    lax.fori_loop(0, seqs, norm_one, 0)
    loads[1].wait()
    loads[2].wait()

    def beside(ref, lanes):
        return jnp.concatenate(
            [ref[s * length:(s + 1) * length, lanes] for s in range(seqs)], axis=1
        )

    tile = 2 * length

    def project_v(r, c):
        at = aligned(r, tile)
        rv[at] = dot(normed[at], hv[...]).astype(BF16)
        return c

    def logits_of(g):
        lanes = slice(g * GROUP, (g + 1) * GROUP)

        def project(r, c):
            at = aligned(r, tile)
            a = normed[at]
            slot = lax.broadcasted_iota(jnp.int32, (tile, 1), 0)
            first = me * seqs + r * 2
            live = jnp.where(
                jnp.where(slot < length, first, first + 1) < count, 1.0, 0.0
            ).astype(F32)
            rq[at, lanes] = (dot(a, hq[:, lanes]) * live).astype(BF16)
            rk[at, lanes] = dot(a, hk[:, lanes]).astype(BF16)
            return c

        lax.fori_loop(0, rows // tile, project, 0)
        for p in range(GROUP // PAIR):
            two = slice(g * GROUP + p * PAIR, g * GROUP + (p + 1) * PAIR)
            q = beside(rq, two)
            q2 = jnp.concatenate([q * left_s, q * right_s], axis=0)
            part[g, p * tile:(p + 1) * tile, :] = dot_t(q2, beside(rk, two)).astype(BF16)
        if g == 0:
            pl.semaphore_wait(barrier, n - 1)
        near(lambda j: rs_copy(g, j).start())

    def exchange(g):
        def add(j, total):
            rs_copy(g, j).wait_recv()
            return total + part_in[g, j].astype(F32)

        mine = part[g, aligned(place_of_me, share), :].astype(F32)
        half_sum[g] = lax.fori_loop(1, half, add, mine).astype(BF16)
        ex_copy(g).start()

    def weigh(g):
        ex_copy(g).wait_recv()
        logits = half_sum[g].astype(F32) + half_in[g].astype(F32)
        weights[g, aligned(place_of_me, share), :] = softmax(logits * inverse)
        near(lambda j: ag_copy(g, j, me).start())

    for g in range(groups):
        logits_of(g)
        if g > 0:
            exchange(g - 1)
    loads[3].wait()
    lax.fori_loop(0, rows // tile // 2, project_v, 0)
    exchange(groups - 1)
    weigh(0)
    lax.fori_loop(rows // tile // 2, rows // tile, project_v, 0)
    for g in range(1, groups):
        weigh(g)

    for g in range(groups):
        near(lambda j: ag_copy(g, j, source(half + j)).wait_recv())
        for p in range(GROUP // PAIR):
            lanes = slice(g * GROUP + p * PAIR, g * GROUP + (p + 1) * PAIR)
            w2 = jnp.concatenate(
                [weights[g, (2 * p + i) * length:(2 * p + i + 1) * length, :] for i in range(2)],
                axis=1,
            )
            v = beside(rv, lanes)
            mixed = dot(w2, jnp.concatenate([v * left_s, v * right_s], axis=0))
            for s in range(seqs):
                live = jnp.where(me * seqs + s < count, 1.0, 0.0).astype(F32)
                row_out[s, :, lanes] = (mixed[:, s * PAIR:(s + 1) * PAIR] * live).astype(BF16)

    row_copy = pltpu.make_async_copy(row_out, row_hbm, load_sem.at[len(loads)])
    row_copy.start()

    loads[4].wait()

    def go_step(t, c):
        at = aligned(t, step_columns)
        a = x[:, at, :].astype(F32) + row_out[:, at, :].astype(F32)
        a = standardize(a).astype(BF16).reshape(seqs * step_columns, width)
        send[t] = dot(there[...], a).astype(BF16)
        each(lambda k: go_copy(t, k, me).start())
        own = aligned(me, step_rows)
        arrived[t, own, :] = send[t, own, :]
        return c

    lax.fori_loop(0, steps, go_step, 0)
    for load in loads[5:]:
        load.wait()

    shift = seqs.bit_length() - 1
    shape = (2 * span, span)

    def place(index):
        return lax.shift_left(lax.shift_right_logical(index, shift + 1), shift) + (index & (seqs - 1))

    def column(index):
        return lax.shift_right_logical(index, shift) & 1

    key = lax.broadcasted_iota(jnp.int32, shape, 1)
    query = lax.broadcasted_iota(jnp.int32, shape, 0)
    open_f = jnp.where(
        (column(key) == column(query)) & (place(key) < count), 1.0, 0.0
    )
    live_q = jnp.where(
        place(lax.broadcasted_iota(jnp.int32, (span, 1), 0)) < count, 1.0, 0.0
    ).astype(F32)

    def attend_step(t, c):
        each(lambda k: go_copy(t, k, source(k)).wait_recv())
        a = arrived[t].reshape(n, step_rows, width)
        a = jnp.concatenate(
            [
                a[:, p * pair_rows:(p + 1) * pair_rows, :].reshape(span, width)
                for p in range(step_pairs)
            ],
            axis=0,
        )
        cq[...] = (dot(a, vq[...]) * (DH ** -0.5)).astype(BF16)
        ck[...] = dot(a, vk[...]).astype(BF16)
        cv[...] = dot(a, vv[...]).astype(BF16)

        def attend_pair(p, c):
            at = aligned(p, span)
            out_at = aligned(p, pair_rows)
            for h in range(width // PAIR):
                lanes = slice(h * PAIR, (h + 1) * PAIR)
                q = cq[at, lanes]
                scores = dot_t(jnp.concatenate([q * left, q * right], axis=0), ck[at, lanes])
                w = softmax(jnp.where(open_f > 0.5, scores, -1e30))
                w2 = jnp.concatenate([w[:span], w[span:]], axis=1)
                v = cv[at, lanes]
                o = dot(w2, jnp.concatenate([v * left, v * right], axis=0))
                ret[t, :, out_at, lanes] = (o * live_q).astype(BF16).reshape(n, pair_rows, PAIR)
            return c

        lax.fori_loop(0, step_pairs, attend_pair, 0)
        each(lambda k: re_copy(t, k, me).start())
        ret_in[t, aligned(me, step_rows), :] = ret[t, me]
        return c

    lax.fori_loop(0, steps, attend_step, 0)

    def col_copy(t):
        at = aligned(t, step_columns)
        return pltpu.make_async_copy(
            out.at[:, at, :], col_hbm.at[:, at, :], load_sem.at[len(loads) + 1 + t]
        )

    def finish(t, c):
        each(lambda k: re_copy(t, k, source(k)).wait_recv())
        out[:, aligned(t, step_columns), :] = (
            dot(back[...], ret_in[t]).astype(BF16).reshape(seqs, step_columns, width)
        )
        col_copy(t).start()
        return c

    lax.fori_loop(0, steps, finish, 0)

    for g in range(groups):
        near(lambda j: rs_copy(g, j).wait_send())
        ex_copy(g).wait_send()
        near(lambda j: ag_copy(g, j, me).wait_send())

    def sent(t, c):
        each(lambda k: go_copy(t, k, me).wait_send())
        each(lambda k: re_copy(t, k, me).wait_send())
        col_copy(t).wait()
        return c

    lax.fori_loop(0, steps, sent, 0)
    row_copy.wait()


def hand_on(*refs):
    sources, results = refs[:2], refs[2:4]
    held, in_sem, out_sem = refs[4:]
    pieces = [(a, s) for a in range(2) for s in range(sources[0].shape[0])]

    def inward(a, s):
        return pltpu.make_async_copy(sources[a].at[s], held.at[a, s], in_sem.at[a, s])

    def outward(a, s):
        return pltpu.make_async_copy(held.at[a, s], results[a].at[s], out_sem.at[a, s])

    for piece in pieces:
        inward(*piece).start()
    for piece in pieces:
        inward(*piece).wait()
        outward(*piece).start()
    for piece in pieces:
        outward(*piece).wait()


def local(x, tallies, hq, hk, hv, vq, vk, vv):
    seqs, length, width = x.shape
    n = lax.axis_size("seq")
    per = length // n
    groups = width // GROUP
    share = (GROUP // DH) * length // (n // 2)
    step_pairs = min(STEP_PAIRS, per // 2)
    steps = per // 2 // step_pairs
    step_rows = step_pairs * 2 * seqs
    span = n * 2 * seqs
    size = n * step_rows
    order = np.arange(size).reshape(seqs, size // seqs).T.reshape(-1)
    there = np.zeros((size, size), np.float32)
    there[np.arange(size), order] = 1.0
    inverse = 1.0 / (jnp.sqrt(F32(DH)) * jnp.sqrt(tallies.astype(F32)))
    any_spec = pl.BlockSpec(memory_space=pl.ANY)
    smem_spec = pl.BlockSpec(memory_space=pltpu.SMEM)
    rows = seqs * length

    def vmem(*shape):
        return pltpu.VMEM(shape, BF16)

    def dma(*shape):
        return pltpu.SemaphoreType.DMA(shape)

    result = jax.ShapeDtypeStruct(x.shape, BF16)
    row, col = pl.pallas_call(
        functools.partial(kernel, n, seqs, length, width),
        out_shape=(result, result),
        in_specs=[smem_spec, smem_spec] + [any_spec] * 9,
        out_specs=(any_spec, any_spec),
        scratch_shapes=[
            vmem(*x.shape),
            *[vmem(width, width) for _ in range(6)],
            vmem(size, size),
            vmem(size, size),
            vmem(rows, width),
            vmem(rows, width),
            vmem(rows, width),
            vmem(rows, width),
            vmem(groups, (GROUP // DH) * length, length),
            vmem(groups, n // 2, share, length),
            vmem(groups, share, length),
            vmem(groups, share, length),
            vmem(groups, (GROUP // DH) * length, length),
            vmem(*x.shape),
            vmem(steps, size, width),
            vmem(steps, size, width),
            vmem(step_pairs * span, width),
            vmem(step_pairs * span, width),
            vmem(step_pairs * span, width),
            vmem(steps, n, step_rows, width),
            vmem(steps, size, width),
            vmem(*x.shape),
            dma(10 + steps),
            dma(groups, n // 2), dma(groups, n // 2), dma(groups), dma(groups),
            dma(groups, n // 2), dma(groups, n // 2),
            dma(steps, n), dma(steps, n), dma(steps, n), dma(steps, n),
        ],
        compiler_params=pltpu.CompilerParams(
            collective_id=0, has_side_effects=True, vmem_limit_bytes=56 * 1024 * 1024
        ),
    )(tallies, inverse, x, hq, hk, hv, vq, vk, vv, jnp.asarray(there, BF16), jnp.asarray(there.T, BF16))
    return pl.pallas_call(
        hand_on,
        out_shape=(result, result),
        in_specs=[any_spec, any_spec],
        out_specs=(any_spec, any_spec),
        scratch_shapes=[vmem(2, *x.shape), dma(2, seqs), dma(2, seqs)],
    )(row, col)


def solution(mesh):
    in_specs = (P(("aln", "seq"), None, None), P("aln"), P(), P(), P(), P(), P(), P())
    out_specs = (P(("aln", "seq"), None, None), P(("aln", "seq"), None, None))
    return jax.shard_map(local, mesh=mesh, in_specs=in_specs, out_specs=out_specs, check_vma=False)
```

```python
import functools

import jax
import jax.numpy as jnp
import numpy as np
from jax import lax
from jax.experimental import pallas as pl
from jax.experimental.pallas import tpu as pltpu
from jax.sharding import PartitionSpec as P

DH = 64
PAIR = 2 * DH
GROUP = 2 * PAIR
STEP_PAIRS = 2
F32 = jnp.float32
BF16 = jnp.bfloat16
MESH = pl.DeviceIdType.MESH


def standardize(values):
    centre = jnp.mean(values, axis=-1, keepdims=True)
    shifted = values - centre
    spread = jnp.mean(shifted * shifted, axis=-1, keepdims=True)
    return shifted * lax.rsqrt(spread + 1e-05)


def softmax(scores):
    e = jnp.exp(scores - jnp.max(scores, axis=-1, keepdims=True))
    return (e * (1.0 / jnp.sum(e, axis=-1, keepdims=True))).astype(BF16)


def dot(a, b):
    return jnp.dot(a, b, preferred_element_type=F32)


def dot_t(a, b):
    return lax.dot_general(a, b, (((1,), (1,)), ((), ())), preferred_element_type=F32)


def kernel(
    n, seqs, length, width,
    count_ref, inv_ref, x_hbm, hq_hbm, hk_hbm, hv_hbm, vq_hbm, vk_hbm, vv_hbm, there_hbm, back_hbm,
    row_hbm, col_hbm,
    x, hq, hk, hv, vq, vk, vv, there, back,
    normed, rq, rk, rv, part, part_in, half_sum, half_in, weights, row_out,
    send, arrived, cq, ck, cv, ret, ret_in, out,
    load_sem, rs_s, rs_r, ex_s, ex_r, ag_s, ag_r, go_s, go_r, re_s, re_r,
):
    half = n // 2
    per = length // n
    rows = seqs * length
    pair_rows = 2 * seqs
    step_pairs = min(STEP_PAIRS, per // 2)
    steps = per // 2 // step_pairs
    step_rows = step_pairs * pair_rows
    step_columns = n * step_pairs * 2
    span = n * pair_rows
    groups = width // GROUP
    share = (GROUP // DH) * length // half
    me = lax.axis_index("seq")
    side_of_me = me // half
    place_of_me = lax.rem(me, half)
    count = count_ref[0]
    inverse = inv_ref[0]

    loads = [
        pltpu.make_async_copy(src, dst, load_sem.at[at])
        for at, (src, dst) in enumerate(
            [(x_hbm, x), (hq_hbm, hq), (hk_hbm, hk), (hv_hbm, hv), (there_hbm, there),
             (vq_hbm, vq), (vk_hbm, vk), (vv_hbm, vv), (back_hbm, back)]
        )
    ]
    for load in loads[:3]:
        load.start()

    barrier = pltpu.get_barrier_semaphore()

    def greet(k, c):
        pl.semaphore_signal(
            barrier, inc=1, device_id={"seq": lax.rem(me + k, n)}, device_id_type=MESH
        )
        return c

    lax.fori_loop(1, n, greet, 0)

    def target(k):
        side = lax.rem(side_of_me + 1 + k // half, 2)
        return side * half + lax.rem(place_of_me + k, half)

    def source(k):
        side = lax.rem(side_of_me + 1 + k // half, 2)
        return side * half + lax.rem(place_of_me + n - k, half)

    def aligned(index, size):
        return pl.ds(pl.multiple_of(index * size, size), size)

    def remote(src, dst, s, r, to):
        return pltpu.make_async_remote_copy(
            src_ref=src, dst_ref=dst, send_sem=s, recv_sem=r, device_id={"seq": to},
            device_id_type=MESH,
        )

    def each(body):
        def one(k, c):
            body(k)
            return c

        lax.fori_loop(0, half, one, 0)
        lax.fori_loop(half + 1, n, one, 0)

    def near(body):
        def one(j, c):
            body(j)
            return c

        lax.fori_loop(1, half, one, 0)

    def rs_copy(g, j):
        at = aligned(lax.rem(place_of_me + j, half), share)
        return remote(
            part.at[g, at], part_in.at[g, j], rs_s.at[g, j], rs_r.at[g, j], target(half + j)
        )

    def ex_copy(g):
        return remote(half_sum.at[g], half_in.at[g], ex_s.at[g], ex_r.at[g], target(0))

    def ag_copy(g, j, owner):
        at = aligned(lax.rem(owner, half), share)
        return remote(
            weights.at[g, at], weights.at[g, at], ag_s.at[g, j], ag_r.at[g, j], target(half + j)
        )

    def go_copy(t, k, owner):
        return remote(
            send.at[t, aligned(target(k), step_rows)], arrived.at[t, aligned(owner, step_rows)],
            go_s.at[t, k], go_r.at[t, k], target(k),
        )

    def re_copy(t, k, owner):
        return remote(
            ret.at[t, target(k)], ret_in.at[t, aligned(owner, step_rows)],
            re_s.at[t, k], re_r.at[t, k], target(k),
        )

    lane = lax.broadcasted_iota(jnp.int32, (1, PAIR), 1)
    left = jnp.where(lane < DH, 1.0, 0.0).astype(BF16)
    right = jnp.where(lane < DH, 0.0, 1.0).astype(BF16)
    left_s = jnp.concatenate([left] * seqs, axis=1)
    right_s = jnp.concatenate([right] * seqs, axis=1)

    loads[0].wait()

    def norm_one(s, c):
        normed[aligned(s, length)] = standardize(x[s].astype(F32)).astype(BF16)
        return c

    lax.fori_loop(0, seqs, norm_one, 0, unroll=2)
    loads[1].wait()
    loads[2].wait()
    for load in loads[3:]:
        load.start()

    def beside(ref, lanes):
        return jnp.concatenate(
            [ref[s * length:(s + 1) * length, lanes] for s in range(seqs)], axis=1
        )

    tile = 2 * length

    def project_v(r, c):
        at = aligned(r, tile)
        rv[at] = dot(normed[at], hv[...]).astype(BF16)
        return c

    def logits_of(g):
        lanes = slice(g * GROUP, (g + 1) * GROUP)

        def project(r, c):
            at = aligned(r, tile)
            a = normed[at]
            slot = lax.broadcasted_iota(jnp.int32, (tile, 1), 0)
            first = me * seqs + r * 2
            live = jnp.where(
                jnp.where(slot < length, first, first + 1) < count, 1.0, 0.0
            ).astype(F32)
            rq[at, lanes] = (dot(a, hq[:, lanes]) * live).astype(BF16)
            rk[at, lanes] = dot(a, hk[:, lanes]).astype(BF16)
            return c

        lax.fori_loop(0, rows // tile, project, 0, unroll=True)
        for p in range(GROUP // PAIR):
            two = slice(g * GROUP + p * PAIR, g * GROUP + (p + 1) * PAIR)
            q = beside(rq, two)
            q2 = jnp.concatenate([q * left_s, q * right_s], axis=0)
            part[g, p * tile:(p + 1) * tile, :] = dot_t(q2, beside(rk, two)).astype(BF16)
        if g == 0:
            pl.semaphore_wait(barrier, n - 1)
        near(lambda j: rs_copy(g, j).start())

    def exchange(g):
        def add(j, total):
            rs_copy(g, j).wait_recv()
            return total + part_in[g, j].astype(F32)

        mine = part[g, aligned(place_of_me, share), :].astype(F32)
        half_sum[g] = lax.fori_loop(1, half, add, mine).astype(BF16)
        ex_copy(g).start()

    def weigh(g):
        ex_copy(g).wait_recv()
        logits = half_sum[g].astype(F32) + half_in[g].astype(F32)
        weights[g, aligned(place_of_me, share), :] = softmax(logits * inverse)
        near(lambda j: ag_copy(g, j, me).start())

    for g in range(groups):
        logits_of(g)
        if g > 0:
            exchange(g - 1)
    loads[3].wait()
    lax.fori_loop(0, rows // tile // 2, project_v, 0, unroll=True)
    exchange(groups - 1)
    for g in range(groups - 1):
        weigh(g)
    lax.fori_loop(rows // tile // 2, rows // tile, project_v, 0, unroll=True)
    weigh(groups - 1)

    for g in range(groups):
        near(lambda j: ag_copy(g, j, source(half + j)).wait_recv())
        for p in range(GROUP // PAIR):
            lanes = slice(g * GROUP + p * PAIR, g * GROUP + (p + 1) * PAIR)
            w2 = jnp.concatenate(
                [weights[g, (2 * p + i) * length:(2 * p + i + 1) * length, :] for i in range(2)],
                axis=1,
            )
            v = beside(rv, lanes)
            mixed = dot(w2, jnp.concatenate([v * left_s, v * right_s], axis=0))
            for s in range(seqs):
                live = jnp.where(me * seqs + s < count, 1.0, 0.0).astype(F32)
                row_out[s, :, lanes] = (mixed[:, s * PAIR:(s + 1) * PAIR] * live).astype(BF16)

    row_copy = pltpu.make_async_copy(row_out, row_hbm, load_sem.at[len(loads)])
    row_copy.start()

    loads[4].wait()

    def go_step(t, c):
        at = aligned(t, step_columns)
        a = x[:, at, :].astype(F32) + row_out[:, at, :].astype(F32)
        a = standardize(a).astype(BF16).reshape(seqs * step_columns, width)
        send[t] = dot(there[...], a).astype(BF16)
        each(lambda k: go_copy(t, k, me).start())
        own = aligned(me, step_rows)
        arrived[t, own, :] = send[t, own, :]
        return c

    lax.fori_loop(0, steps, go_step, 0)
    for load in loads[5:]:
        load.wait()

    shift = seqs.bit_length() - 1
    shape = (2 * span, span)

    def place(index):
        return lax.shift_left(lax.shift_right_logical(index, shift + 1), shift) + (index & (seqs - 1))

    def column(index):
        return lax.shift_right_logical(index, shift) & 1

    key = lax.broadcasted_iota(jnp.int32, shape, 1)
    query = lax.broadcasted_iota(jnp.int32, shape, 0)
    open_f = jnp.where(
        (column(key) == column(query)) & (place(key) < count), 1.0, 0.0
    )
    live_q = jnp.where(
        place(lax.broadcasted_iota(jnp.int32, (span, 1), 0)) < count, 1.0, 0.0
    ).astype(F32)

    def attend_step(t, c):
        each(lambda k: go_copy(t, k, source(k)).wait_recv())
        a = arrived[t].reshape(n, step_rows, width)
        a = jnp.concatenate(
            [
                a[:, p * pair_rows:(p + 1) * pair_rows, :].reshape(span, width)
                for p in range(step_pairs)
            ],
            axis=0,
        )
        cq[...] = (dot(a, vq[...]) * (DH ** -0.5)).astype(BF16)
        ck[...] = dot(a, vk[...]).astype(BF16)
        cv[...] = dot(a, vv[...]).astype(BF16)

        def attend_pair(p, c):
            at = aligned(p, span)
            out_at = aligned(p, pair_rows)
            for h in range(width // PAIR):
                lanes = slice(h * PAIR, (h + 1) * PAIR)
                q = cq[at, lanes]
                scores = dot_t(jnp.concatenate([q * left, q * right], axis=0), ck[at, lanes])
                w = softmax(jnp.where(open_f > 0.5, scores, -1e30))
                w2 = jnp.concatenate([w[:span], w[span:]], axis=1)
                v = cv[at, lanes]
                o = dot(w2, jnp.concatenate([v * left, v * right], axis=0))
                ret[t, :, out_at, lanes] = (o * live_q).astype(BF16).reshape(n, pair_rows, PAIR)
            return c

        lax.fori_loop(0, step_pairs, attend_pair, 0)
        each(lambda k: re_copy(t, k, me).start())
        ret_in[t, aligned(me, step_rows), :] = ret[t, me]
        return c

    lax.fori_loop(0, steps, attend_step, 0)

    def col_copy(t):
        at = aligned(t, step_columns)
        return pltpu.make_async_copy(
            out.at[:, at, :], col_hbm.at[:, at, :], load_sem.at[len(loads) + 1 + t]
        )

    def finish(t, c):
        each(lambda k: re_copy(t, k, source(k)).wait_recv())
        out[:, aligned(t, step_columns), :] = (
            dot(back[...], ret_in[t]).astype(BF16).reshape(seqs, step_columns, width)
        )
        col_copy(t).start()
        return c

    lax.fori_loop(0, steps, finish, 0)

    for g in range(groups):
        near(lambda j: rs_copy(g, j).wait_send())
        ex_copy(g).wait_send()
        near(lambda j: ag_copy(g, j, me).wait_send())

    def sent(t, c):
        each(lambda k: go_copy(t, k, me).wait_send())
        each(lambda k: re_copy(t, k, me).wait_send())
        col_copy(t).wait()
        return c

    lax.fori_loop(0, steps, sent, 0)
    row_copy.wait()


def hand_on(*refs):
    sources, results = refs[:2], refs[2:4]
    held, in_sem, out_sem = refs[4:]
    pieces = [(a, s) for a in range(2) for s in range(sources[0].shape[0])]

    def inward(a, s):
        return pltpu.make_async_copy(sources[a].at[s], held.at[a, s], in_sem.at[a, s])

    def outward(a, s):
        return pltpu.make_async_copy(held.at[a, s], results[a].at[s], out_sem.at[a, s])

    for piece in pieces:
        inward(*piece).start()
    for piece in pieces:
        inward(*piece).wait()
        outward(*piece).start()
    for piece in pieces:
        outward(*piece).wait()


def local(x, tallies, hq, hk, hv, vq, vk, vv):
    seqs, length, width = x.shape
    n = lax.axis_size("seq")
    per = length // n
    groups = width // GROUP
    share = (GROUP // DH) * length // (n // 2)
    step_pairs = min(STEP_PAIRS, per // 2)
    steps = per // 2 // step_pairs
    step_rows = step_pairs * 2 * seqs
    span = n * 2 * seqs
    size = n * step_rows
    order = np.arange(size).reshape(seqs, size // seqs).T.reshape(-1)
    there = np.zeros((size, size), np.float32)
    there[np.arange(size), order] = 1.0
    inverse = 1.0 / (jnp.sqrt(F32(DH)) * jnp.sqrt(tallies.astype(F32)))
    any_spec = pl.BlockSpec(memory_space=pl.ANY)
    smem_spec = pl.BlockSpec(memory_space=pltpu.SMEM)
    rows = seqs * length

    def vmem(*shape):
        return pltpu.VMEM(shape, BF16)

    def dma(*shape):
        return pltpu.SemaphoreType.DMA(shape)

    result = jax.ShapeDtypeStruct(x.shape, BF16)
    row, col = pl.pallas_call(
        functools.partial(kernel, n, seqs, length, width),
        out_shape=(result, result),
        in_specs=[smem_spec, smem_spec] + [any_spec] * 9,
        out_specs=(any_spec, any_spec),
        scratch_shapes=[
            vmem(*x.shape),
            *[vmem(width, width) for _ in range(6)],
            vmem(size, size),
            vmem(size, size),
            vmem(rows, width),
            vmem(rows, width),
            vmem(rows, width),
            vmem(rows, width),
            vmem(groups, (GROUP // DH) * length, length),
            vmem(groups, n // 2, share, length),
            vmem(groups, share, length),
            vmem(groups, share, length),
            vmem(groups, (GROUP // DH) * length, length),
            vmem(*x.shape),
            vmem(steps, size, width),
            vmem(steps, size, width),
            vmem(step_pairs * span, width),
            vmem(step_pairs * span, width),
            vmem(step_pairs * span, width),
            vmem(steps, n, step_rows, width),
            vmem(steps, size, width),
            vmem(*x.shape),
            dma(10 + steps),
            dma(groups, n // 2), dma(groups, n // 2), dma(groups), dma(groups),
            dma(groups, n // 2), dma(groups, n // 2),
            dma(steps, n), dma(steps, n), dma(steps, n), dma(steps, n),
        ],
        compiler_params=pltpu.CompilerParams(
            collective_id=0, has_side_effects=True, vmem_limit_bytes=56 * 1024 * 1024
        ),
    )(tallies, inverse, x, hq, hk, hv, vq, vk, vv, jnp.asarray(there, BF16), jnp.asarray(there.T, BF16))
    return pl.pallas_call(
        hand_on,
        out_shape=(result, result),
        in_specs=[any_spec, any_spec],
        out_specs=(any_spec, any_spec),
        scratch_shapes=[vmem(2, *x.shape), dma(2, seqs), dma(2, seqs)],
    )(row, col)


def solution(mesh):
    in_specs = (P(("aln", "seq"), None, None), P("aln"), P(), P(), P(), P(), P(), P())
    out_specs = (P(("aln", "seq"), None, None), P(("aln", "seq"), None, None))
    return jax.shard_map(local, mesh=mesh, in_specs=in_specs, out_specs=out_specs, check_vma=False)
```
